512 devices in a mesh: gx: 16 (over y, z_hi), gz: 32 (over x, z_lo, core).
Axes of the slice: x: 4, y: 8, z: 8 (z_hi: 2, z_lo: 4; z = z_hi * 4 + z_lo), core: 2. Of those that a mesh axis runs over, the one named last changes fastest.
Arguments:
- pressure: float32 [256, 512, 512], P('gx', 'gz'), may hold values from -6 to 6
- previous: float32 [256, 512, 512], P('gx', 'gz'), may hold values from -6 to 6
- states: float32 [16, 32, 256, 128], P('gx', 'gz'), may hold values from -4 to 4
- wall_cell: int32 [16, 32, 256], P('gx', 'gz'), may hold values from 0 to 131071, as said below
- wall_count: int32 [16, 32], P('gx', 'gz'), may hold values from 64 to 256, as said below
- material: int32 [16, 32, 256], P('gx', 'gz'), may hold values from 0 to 3
- partner: int32 [16, 32, 256], P('gx', 'gz'), may hold values from 0 to 1279
- transitions: float32 [4, 128, 128], replicated
- inputs: float32 [4, 128], replicated, may hold values from -4 to 4
- outputs: float32 [4, 128], replicated, may hold values from -0.5 to 0.5
Outputs:
- pressure_out: float32 [256, 512, 512], P('gx', 'gz')
- states_out: float32 [16, 32, 256, 128], P('gx', 'gz')
The draws below stay inside these ranges and needn't reach their ends.
Inputs may be any that keep to these rules, and one draw needn't show every extreme that they name: `wall_cell`: within one device block the wall cells of all slots are distinct; slot k lies in the k-th of 256 equal runs of the block's flattened cells. `wall_count`: some device holds 256 live slots in every draw.
All inputs are finite; a program needn't handle non-finite values.
Results may differ from the reference program's by a relative error of at most 0.00026.
Values sent between devices are 32-bit elements; how exact they have to be, the bound alone decides.
A program may use at most 64 MiB of HBM per device.

```python
import jax
import jax.numpy as jnp
from jax import lax

CX = 16
CZ = 16
NY = 512
W = 256
FILT = 128
MAT = 4
STEPS = 3
NX = 256
NZ = 512
N_GX = 16
N_GZ = 32


def draw_wall_cell(key, part):
    key = jax.random.fold_in(key, 11)
    run = CX * CZ * NY // W
    offset = jax.random.randint(key, (N_GX, N_GZ, W), 0, run)
    return (jnp.arange(W, dtype=jnp.int32)[None, None, :] * run + offset).astype(jnp.int32)


def draw_wall_count(key, part):
    key = jax.random.fold_in(key, 12)
    first, second = jax.random.split(key)
    counts = jax.random.randint(first, (N_GX * N_GZ,), W // 4, W + 1)
    chosen = jax.random.randint(second, (), 0, N_GX * N_GZ)
    counts = jnp.where(jnp.arange(N_GX * N_GZ) == chosen, W, counts)
    return counts.reshape(N_GX, N_GZ).astype(jnp.int32)


def draw_transitions(key, part):
    key = jax.random.fold_in(key, 13)
    first, second = jax.random.split(key)
    diag = jnp.exp(jax.random.uniform(first, (MAT, FILT), jnp.float32, jnp.log(0.3), jnp.log(0.9)))
    off = jax.random.normal(second, (MAT, FILT, FILT), jnp.float32) * (0.15 / FILT ** 0.5)
    return (off + diag[:, :, None] * jnp.eye(FILT, dtype=jnp.float32)[None]).astype(jnp.float32)


def set_ends(drawn, stream_key, least, high):
    spot = [jax.random.randint(jax.random.fold_in(stream_key, axis), (), 0, length) for axis, length in enumerate(drawn.shape)]
    widest = drawn.shape.index(max(drawn.shape))
    next_to = spot[:widest] + [(spot[widest] + 1) % drawn.shape[widest]] + spot[widest + 1:]
    return drawn.at[tuple(spot)].set(least).at[tuple(next_to)].set(high)


def level_of(stream_key, shape, cuts, low, high):
    loudness, own = 1.0, jax.random.fold_in(stream_key, 6)
    for dim, parts in cuts:
        heights = jnp.exp(jax.random.uniform(jax.random.fold_in(own, dim), (parts,), jnp.float32, low / len(cuts), high / len(cuts)))
        loudness = loudness * jnp.repeat(heights, shape[dim] // parts).reshape([-1 if axis == dim else 1 for axis in range(len(shape))])
    return loudness


def gaussian(own_key, dims, width, most, shards=(), kind=jnp.bfloat16):
    result = jax.random.normal(own_key, dims, jnp.float32) * width
    if len(shards) > 0:
        result = level_of(own_key, dims, shards, -0.22, 0.18) * result
    return jnp.clip(result, min=-most, max=most).astype(kind)


def setup_inputs(seed: int = 0) -> dict:
    arg_keys = jax.random.split(jax.random.key(seed), 11)
    pressure = gaussian(arg_keys[0], (NX, NZ, NY), 1.0, 6.0, ((0, 16), (1, 32)), jnp.float32)
    previous = gaussian(arg_keys[1], (NX, NZ, NY), 1.0, 6.0, ((0, 16), (1, 32)), jnp.float32)
    states = gaussian(arg_keys[2], (N_GX, N_GZ, W, FILT), 0.5, 4.0, ((0, 16), (1, 32)), jnp.float32)
    wall_cell = draw_wall_cell(jax.random.fold_in(arg_keys[10], 71), 0)
    wall_count = draw_wall_count(jax.random.fold_in(arg_keys[10], 71), 0)
    material = set_ends(jax.random.randint(arg_keys[5], (N_GX, N_GZ, W), 0, MAT), jax.random.fold_in(arg_keys[5], 1), 0, MAT - 1).astype(jnp.int32)
    partner = set_ends(jax.random.randint(arg_keys[6], (N_GX, N_GZ, W), 0, 5 * W), jax.random.fold_in(arg_keys[6], 1), 0, (5 * W) - 1).astype(jnp.int32)
    transitions = draw_transitions(jax.random.fold_in(arg_keys[10], 71), 0)
    inputs = gaussian(arg_keys[8], (MAT, FILT), 0.5, 4.0, (), jnp.float32)
    outputs = gaussian(arg_keys[9], (MAT, FILT), FILT ** -0.5, 0.5, (), jnp.float32)
    return dict(pressure=pressure, previous=previous, states=states, wall_cell=wall_cell, wall_count=wall_count, material=material, partner=partner, transitions=transitions, inputs=inputs, outputs=outputs)


face_w = 0.5
edge_w = 0.0625
corner_w = 0.0625
courant = 0.3
coupling = 0.3


def weight_of(first, second, third):
    count = abs(first) + abs(second) + abs(third)
    return [-(6 * face_w + 12 * edge_w + 8 * corner_w), face_w, edge_w, corner_w][count]


def laplace(padded, shape):
    total = jnp.zeros(shape, jnp.float32)
    for first in (-1, 0, 1):
        for second in (-1, 0, 1):
            for third in (-1, 0, 1):
                piece = padded[1 + first:1 + first + shape[0], 1 + second:1 + second + shape[1], 1 + third:1 + third + shape[2]]
                total = total + weight_of(first, second, third) * piece
    return total


def reference(pressure, previous, states, wall_cell, wall_count, material, partner, transitions, inputs, outputs):
    highest = lax.Precision.HIGHEST
    shape = pressure.shape
    live = (jnp.arange(W, dtype=jnp.int32)[None, None, :] < wall_count[:, :, None]).astype(jnp.float32)
    row_i = jnp.arange(N_GX, dtype=jnp.int32)[:, None, None]
    col_j = jnp.arange(N_GZ, dtype=jnp.int32)[None, :, None]
    glob_x = row_i * CX + wall_cell // (CZ * NY)
    glob_z = col_j * CZ + (wall_cell // NY) % CZ
    glob_y = wall_cell % NY
    flat = ((glob_x * NZ + glob_z) * NY + glob_y).reshape(-1).astype(jnp.int32)
    onehot = (material[..., None] == jnp.arange(MAT, dtype=jnp.int32)).astype(jnp.float32)
    drive = jnp.einsum('gzwm,mf->gzwf', onehot, inputs, precision=highest)
    readout = jnp.einsum('gzwm,mf->gzwf', onehot, outputs, precision=highest)
    state = states * live[..., None]
    for step in range(STEPS):
        lap = laplace(jnp.pad(pressure, 1), shape)
        following = 2.0 * pressure - previous + courant * lap
        velocity = (pressure.reshape(-1)[flat] - previous.reshape(-1)[flat]).reshape(N_GX, N_GZ, W)
        padded = jnp.pad(state, ((1, 1), (1, 1), (0, 0), (0, 0)))
        cand = jnp.concatenate([padded[1:-1, 1:-1], padded[:-2, 1:-1], padded[2:, 1:-1], padded[1:-1, :-2], padded[1:-1, 2:]], axis=2)
        partner_state = jnp.take_along_axis(cand, partner[..., None], axis=2)
        moved = jnp.einsum('gzwf,mfh->gzwmh', state, transitions, precision=highest)
        mixed = jnp.einsum('gzwm,gzwmh->gzwh', onehot, moved, precision=highest)
        new = (mixed + velocity[..., None] * drive + coupling * (partner_state - state)) * live[..., None]
        correction = jnp.sum(new * readout, axis=-1) * live
        following = following.reshape(-1).at[flat].add(-correction.reshape(-1)).reshape(shape)
        previous, pressure, state = pressure, following, new
    return pressure, state
```

```python
import functools

import jax
import jax.numpy as jnp
from jax import lax
from jax.experimental import pallas as pl
from jax.experimental.pallas import tpu as pltpu
from jax.sharding import PartitionSpec as P

MESH = pl.DeviceIdType.MESH
STEPS = 3
CHUNKS = 4
MIRROR, OTHER, BEFORE, AFTER = range(4)

face_w = 0.5
edge_w = 0.0625
corner_w = 0.0625
centre_w = -(6 * face_w + 12 * edge_w + 8 * corner_w)
courant = 0.3
coupling = 0.3


def split(value):
    high = value.astype(jnp.bfloat16)
    low = (value - high.astype(jnp.float32)).astype(jnp.bfloat16)
    return high, low


def dot(left, right):
    return jnp.dot(left, right, preferred_element_type=jnp.float32)


def kernel(
    sizes,
    p_ref,
    q_ref,
    s_ref,
    cell_ref,
    count_ref,
    material_ref,
    partner_ref,
    transition_ref,
    input_ref,
    output_ref,
    p_out,
    s_out,
    state,
    found,
    gather,
    mix_a,
    mix_b,
    drive,
    readout,
    mask,
    p_mid,
    halo_x,
    halo_z,
    halo_c,
    face_z,
    face_c,
    beside,
    free,
    picked,
    s_send,
    s_recv,
    p_send,
    p_recv,
):
    n_gx, n_gz = sizes
    cx, cz, ny = p_ref.shape
    slots, filt = s_ref.shape
    kinds = transition_ref.shape[0]
    rows = filt // CHUNKS
    lanes = 128
    i, j = lax.axis_index("gx"), lax.axis_index("gz")
    upper = lax.rem(i, 2)
    has_xm, has_xp = i > 0, i < n_gx - 1
    has_zm, has_zp = j > 0, j < n_gz - 1
    mirror = (i + 1 - 2 * upper, j)
    relay_to = (i + 2 - 4 * upper, j)
    has_mirror = jnp.logical_or(upper == 1, has_xp)
    other_at = i - 1 + 2 * upper
    has_other = jnp.logical_and(other_at >= 0, other_at < n_gx)
    can_relay = jnp.logical_and(
        jnp.logical_and(relay_to[0] >= 0, relay_to[0] < n_gx), has_mirror
    )

    near = {}
    for dx in (-1, 0, 1):
        for dz in (-1, 0, 1):
            if dx or dz:
                present = [has_xm, None, has_xp][dx + 1], [has_zm, None, has_zp][dz + 1]
                present = [one for one in present if one is not None]
                near[dx, dz] = (functools.reduce(jnp.logical_and, present), (i + dx, j + dz))
    greeted = list(near.values()) + [(i >= 2, (i - 2, j)), (i < n_gx - 2, (i + 2, j))]

    barrier = pltpu.get_barrier_semaphore()
    for present, device in greeted:

        @pl.when(present)
        def _():
            pl.semaphore_signal(barrier, inc=1, device_id=device, device_id_type=MESH)

    state[0] = jnp.transpose(s_ref[...]) * (
        lax.broadcasted_iota(jnp.int32, (filt, slots), 1) < count_ref[0, 0]
    ).astype(jnp.float32)
    live = (lax.broadcasted_iota(jnp.int32, (1, slots), 1) < count_ref[0, 0]).astype(jnp.float32)

    expected = functools.reduce(
        lambda a, b: a + b, [present.astype(jnp.int32) for present, _ in greeted]
    )

    def remote(src, dst, send, recv, device):
        return pltpu.make_async_remote_copy(
            src_ref=src, dst_ref=dst, send_sem=send, recv_sem=recv, device_id=device, device_id_type=MESH
        )

    def piece(c):
        return pl.ds(c * rows, rows)

    def s_copy(t, way, c):
        src = found.at[t, MIRROR, piece(c)] if way == OTHER else state.at[t, piece(c)]
        device = [mirror, relay_to, (i, j + 1), (i, j - 1)][way]
        return remote(src, found.at[t, way, piece(c)], s_send.at[t, way, c], s_recv.at[t, way, c], device)

    s_goes = [has_mirror, can_relay, has_zp, has_zm]
    s_comes = [has_mirror, has_other, has_zm, has_zp]

    def send_state(t, c):
        for way in (MIRROR, BEFORE, AFTER):
            pl.when(s_goes[way])(s_copy(t, way, c).start)

    def relay(t, c):
        pl.when(has_mirror)(s_copy(t, MIRROR, c).wait_recv)
        pl.when(can_relay)(s_copy(t, OTHER, c).start)

    def p_at(t):
        return p_ref if t == 0 else p_mid.at[t - 1]

    corner_of = {(-1, -1): 0, (-1, 1): 1, (1, -1): 2, (1, 1): 3}

    def p_copies(t):
        copies = []
        for k, ((dx, dz), (present, device)) in enumerate(near.items()):
            if dz == 0:
                src = p_at(t).at[cx - 1 if dx > 0 else 0]
                dst = halo_x.at[t, 0 if dx > 0 else 1]
            elif dx == 0:
                src = face_z.at[t, 1 if dz > 0 else 0]
                dst = halo_z.at[t, 0 if dz > 0 else 1]
            else:
                src = face_c.at[t, corner_of[dx, dz]]
                dst = halo_c.at[t, corner_of[-dx, -dz]]
            copies.append(
                (present, near[-dx, -dz][0], remote(src, dst, p_send.at[t, k], p_recv.at[t, k], device))
            )
        return copies

    def stage_faces(t):
        for x in range(cx):
            face_z[t, 0, x : x + 1, :] = p_at(t)[x, 0:1, :]
            face_z[t, 1, x : x + 1, :] = p_at(t)[x, cz - 1 : cz, :]
        for (dx, dz), k in corner_of.items():
            face_c[t, k] = p_at(t)[cx - 1 if dx > 0 else 0, (cz - 1 if dz > 0 else 0) :][0:1, :]

    def send_faces(t):
        stage_faces(t)
        for goes, _, copy in p_copies(t):
            pl.when(goes)(copy.start)

    for way, present in enumerate(s_comes):

        @pl.when(jnp.logical_not(present))
        def _():
            for t in range(STEPS):
                found[t, way] = jnp.zeros((filt, slots), jnp.float32)

    for (dx, dz), (present, _) in near.items():

        @pl.when(jnp.logical_not(present))
        def _():
            for t in range(STEPS):
                if dz == 0:
                    halo_x[t, 0 if dx < 0 else 1] = jnp.zeros((cz, ny), jnp.float32)
                elif dx == 0:
                    halo_z[t, 0 if dz < 0 else 1] = jnp.zeros((cx, ny), jnp.float32)
                else:
                    halo_c[t, corner_of[dx, dz]] = jnp.zeros((1, ny), jnp.float32)

    pl.semaphore_wait(barrier, expected)
    for c in range(CHUNKS):
        send_state(0, c)
    send_faces(0)

    way_code = [0, 2 - upper, 1 + upper, 3, 4]
    slot_down = lax.broadcasted_iota(jnp.int32, (slots, slots), 0)
    for d, code in enumerate(way_code):
        gather[d] = (slot_down + code * slots == partner_ref[...]).astype(jnp.float32).astype(jnp.bfloat16)
    kind = [(material_ref[...] == m).astype(jnp.float32) for m in range(kinds)]
    in_t = jnp.transpose(jnp.concatenate([input_ref[...], output_ref[...]], axis=0))
    drive[...] = functools.reduce(lambda a, b: a + b, [in_t[:, m : m + 1] * kind[m] for m in range(kinds)])
    readout[...] = functools.reduce(
        lambda a, b: a + b, [in_t[:, kinds + m : kinds + m + 1] * kind[m] for m in range(kinds)]
    )
    for m in range(kinds):
        high, low = split(jnp.transpose(transition_ref[m]))
        here = slice(m * filt, (m + 1) * filt)
        mix_a[here, 0:filt] = high
        mix_a[here, filt : 2 * filt] = high
        mix_b[here, :] = low
    along = lax.rem(cell_ref[...], ny).astype(jnp.float32)
    place = jnp.transpose(jnp.broadcast_to(along, (lanes, slots)))
    lane = lax.broadcasted_iota(jnp.int32, (cz, lanes), 1).astype(jnp.float32)
    for x in range(cx):
        for part in range(ny // lanes):
            mask[x, :, part * lanes : (part + 1) * lanes] = (
                place[x * cz : (x + 1) * cz] == lane + float(part * lanes)
            ).astype(jnp.float32)

    def pick(x, change):
        chosen = mask[x] * change
        picked[pl.ds(x * cz, cz), :] = functools.reduce(
            lambda a, b: a + b, [chosen[:, k * lanes : (k + 1) * lanes] for k in range(ny // lanes)]
        )

    def picked_row():
        return jnp.sum(jnp.transpose(picked[...]), axis=0, keepdims=True)

    def first_change(x, _):
        pick(x, p_ref[x] - q_ref[x])
        return 0

    lax.fori_loop(0, cx, first_change, 0)
    velocity = picked_row()

    iota_z = lax.broadcasted_iota(jnp.int32, (cz, ny), 0)
    iota_y = lax.broadcasted_iota(jnp.int32, (cz, ny), 1)
    rest_w = face_w - edge_w

    def both_y(value):
        return jnp.where(iota_y == 0, 0.0, pltpu.roll(value, 1, 1)) + jnp.where(
            iota_y == ny - 1, 0.0, pltpu.roll(value, ny - 1, 1)
        )

    def plane(here, low, high):
        both_z = jnp.where(iota_z == 0, low, pltpu.roll(here, 1, 0)) + jnp.where(
            iota_z == cz - 1, high, pltpu.roll(here, cz - 1, 0)
        )
        line = edge_w * (here + both_z)
        side = line + both_y(line) + rest_w * here
        return line, both_z, side

    def pressure_free(t):
        for _, comes, copy in p_copies(t):
            pl.when(comes)(copy.wait_recv)
        now, before = p_at(t), (q_ref if t == 0 else p_at(t - 1))
        for end in (0, 1):
            low, high = halo_c[t, corner_of[2 * end - 1, -1]], halo_c[t, corner_of[2 * end - 1, 1]]
            beside[0 if end == 0 else cx + 1] = plane(halo_x[t, end], low, high)[2]

        def inner(x, _):
            here = now[x]
            low, high = halo_z[t, 0, pl.ds(x, 1), :], halo_z[t, 1, pl.ds(x, 1), :]
            line, both_z, side = plane(here, low, high)
            beside[x + 1] = side
            own = (
                line
                + both_y(line + rest_w * here)
                + rest_w * both_z
                + (centre_w - edge_w) * here
            )
            free[x] = 2.0 * here - before[x] + courant * own
            return 0

        lax.fori_loop(0, cx, inner, 0)

        def finish(x, _):
            value = free[x] + courant * (beside[x] + beside[x + 2])
            free[x] = value
            pick(x, value - now[x])
            return 0

        lax.fori_loop(0, cx, finish, 0)
        return picked_row()

    for t in range(STEPS):
        now = state[t]
        high, low = split(now)
        stacked = jnp.concatenate([high, low], axis=0)
        moved = dot(mix_a[...], stacked) + dot(mix_b[...], high)
        base = functools.reduce(
            lambda a, b: a + b, [moved[m * filt : (m + 1) * filt] * kind[m] for m in range(kinds)]
        )
        own = dot(stacked, gather[0])
        base = base + velocity * drive[...] + coupling * (own[:filt] + own[filt:] - now)
        relay(t, 0)
        for c in range(CHUNKS):
            if c + 1 < CHUNKS:
                relay(t, c + 1)
            total = base[c * rows : (c + 1) * rows]
            for way in (MIRROR, BEFORE, AFTER, OTHER):
                if way != MIRROR:
                    pl.when(s_comes[way])(s_copy(t, way, c).wait_recv)
                high, low = split(found[t, way, piece(c)])
                got = dot(jnp.concatenate([high, low], axis=0), gather[way + 1])
                total = total + coupling * (got[:rows] + got[rows:])
            state[t + 1, piece(c)] = total * live
            if t + 1 < STEPS:
                send_state(t + 1, c)
        change = pressure_free(t)
        product = state[t + 1] * readout[...]
        correction = jnp.sum(product, axis=0, keepdims=True)
        velocity = change - correction
        column = jnp.sum(jnp.transpose(product), axis=1, keepdims=True)
        for x in range(cx):
            value = free[x] - column[x * cz : (x + 1) * cz] * mask[x]
            if t + 1 < STEPS:
                p_mid[t, x] = value
            else:
                p_out[x] = value
        if t + 1 < STEPS:
            send_faces(t + 1)
    s_out[...] = jnp.transpose(state[STEPS])

    for t in range(STEPS):
        for way, goes in enumerate(s_goes):

            @pl.when(goes)
            def _():
                for c in range(CHUNKS):
                    s_copy(t, way, c).wait_send()

        for goes, _, copy in p_copies(t):
            pl.when(goes)(copy.wait_send)


def per_device(
    pressure,
    previous,
    states,
    wall_cell,
    wall_count,
    material,
    partner,
    transitions,
    inputs,
    outputs,
):
    cx, cz, ny = pressure.shape
    slots, filt = states.shape[2:]
    kinds = transitions.shape[0]
    sizes = (lax.axis_size("gx"), lax.axis_size("gz"))
    f32, bf16 = jnp.float32, jnp.bfloat16
    vmem = pl.BlockSpec(memory_space=pltpu.VMEM)
    smem = pl.BlockSpec(memory_space=pltpu.SMEM)
    pressure_out, states_out = pl.pallas_call(
        functools.partial(kernel, sizes),
        out_shape=[
            jax.ShapeDtypeStruct((cx, cz, ny), f32),
            jax.ShapeDtypeStruct((slots, filt), f32),
        ],
        in_specs=[vmem, vmem, vmem, vmem, smem, vmem, vmem, vmem, vmem, vmem],
        out_specs=[vmem, vmem],
        scratch_shapes=[
            pltpu.VMEM((STEPS + 1, filt, slots), f32),
            pltpu.VMEM((STEPS, 4, filt, slots), f32),
            pltpu.VMEM((5, slots, slots), bf16),
            pltpu.VMEM((kinds * filt, 2 * filt), bf16),
            pltpu.VMEM((kinds * filt, filt), bf16),
            pltpu.VMEM((filt, slots), f32),
            pltpu.VMEM((filt, slots), f32),
            pltpu.VMEM((cx, cz, ny), f32),
            pltpu.VMEM((STEPS - 1, cx, cz, ny), f32),
            pltpu.VMEM((STEPS, 2, cz, ny), f32),
            pltpu.VMEM((STEPS, 2, cx, ny), f32),
            pltpu.VMEM((STEPS, 4, 1, ny), f32),
            pltpu.VMEM((STEPS, 2, cx, ny), f32),
            pltpu.VMEM((STEPS, 4, 1, ny), f32),
            pltpu.VMEM((cx + 2, cz, ny), f32),
            pltpu.VMEM((cx, cz, ny), f32),
            pltpu.VMEM((slots, 128), f32),
            pltpu.SemaphoreType.DMA((STEPS, 4, CHUNKS)),
            pltpu.SemaphoreType.DMA((STEPS, 4, CHUNKS)),
            pltpu.SemaphoreType.DMA((STEPS, 8)),
            pltpu.SemaphoreType.DMA((STEPS, 8)),
        ],
        compiler_params=pltpu.CompilerParams(
            collective_id=0, has_side_effects=True, vmem_limit_bytes=40 * 1024 * 1024
        ),
        name="leapfrog",
    )(
        pressure,
        previous,
        states.reshape(slots, filt),
        wall_cell.reshape(1, slots),
        wall_count,
        material.reshape(1, slots),
        partner.reshape(1, slots),
        transitions,
        inputs,
        outputs,
    )
    return pressure_out, states_out.reshape(1, 1, slots, filt)


def solution(mesh):
    placed = (
        P("gx", "gz", None),
        P("gx", "gz", None),
        P("gx", "gz", None, None),
        P("gx", "gz", None),
        P("gx", "gz"),
        P("gx", "gz", None),
        P("gx", "gz", None),
        P(),
        P(),
        P(),
    )
    return jax.shard_map(
        per_device,
        mesh=mesh,
        in_specs=placed,
        out_specs=(P("gx", "gz", None), P("gx", "gz", None, None)),
        check_vma=False,
    )
```

```python
import functools

import jax
import jax.numpy as jnp
from jax import lax
from jax.experimental import pallas as pl
from jax.experimental.pallas import tpu as pltpu
from jax.sharding import PartitionSpec as P

MESH = pl.DeviceIdType.MESH
STEPS = 3
CHUNKS = 2
PRESSURE_AT = (0, 1, 1)
SEND_ORDER = 2
OTHER, BEFORE, AFTER = range(3)
OWN, MIRROR = range(2)

face_w = 0.5
edge_w = 0.0625
corner_w = 0.0625
centre_w = -(6 * face_w + 12 * edge_w + 8 * corner_w)
courant = 0.3
coupling = 0.3


def split(value):
    high = value.astype(jnp.bfloat16)
    low = (value - high.astype(jnp.float32)).astype(jnp.bfloat16)
    return high, low


def dot(left, right):
    return jnp.dot(left, right, preferred_element_type=jnp.float32)


def kernel(
    sizes,
    p_hbm,
    q_hbm,
    s_hbm,
    cell_hbm,
    count_ref,
    material_hbm,
    partner_hbm,
    transition_hbm,
    input_hbm,
    output_hbm,
    p_out,
    s_out,
    q_ref,
    s_ref,
    cell_ref,
    material_ref,
    partner_ref,
    transition_ref,
    input_ref,
    output_ref,
    state,
    found,
    base,
    info_out,
    info_in,
    v_out,
    v_in,
    kind,
    gather,
    mix_a,
    mix_b,
    drive,
    readout,
    mask,
    pressure,
    halo_z,
    halo_c,
    face_z,
    face_c,
    edge_out,
    edge_in,
    turned,
    column,
    free,
    picked,
    load_sem,
    store_sem,
    info_sem,
    x_send,
    x_recv,
    v_send,
    v_recv,
    s_send,
    s_recv,
    p_send,
    p_recv,
    e_send,
    e_recv,
):
    n_gx, n_gz = sizes
    cx, cz, ny = q_ref.shape
    slots, filt = s_ref.shape
    kinds = transition_ref.shape[0]
    rows = filt // CHUNKS
    lanes = 128
    parts = ny // lanes
    i, j = lax.axis_index("gx"), lax.axis_index("gz")
    upper = lax.rem(i, 2)
    has_xm, has_xp = i > 0, i < n_gx - 1
    has_zm, has_zp = j > 0, j < n_gz - 1
    mirror = (i + 1 - 2 * upper, j)
    up_to, down_to = (i + 2 - 4 * upper, j), (i - 2 + 4 * upper, j)
    has_up = jnp.logical_and(up_to[0] >= 0, up_to[0] < n_gx)
    has_down = jnp.logical_and(down_to[0] >= 0, down_to[0] < n_gx)

    near = {}
    for dx in (-1, 0, 1):
        for dz in (-1, 0, 1):
            if dx or dz:
                present = [has_xm, None, has_xp][dx + 1], [has_zm, None, has_zp][dz + 1]
                present = [one for one in present if one is not None]
                near[dx, dz] = (functools.reduce(jnp.logical_and, present), (i + dx, j + dz))
    order = {way: k for k, way in enumerate(near)}
    corner_of = {(-1, -1): 0, (-1, 1): 1, (1, -1): 2, (1, 1): 3}
    greeted = list(near.values()) + [(i >= 2, (i - 2, j)), (i < n_gx - 2, (i + 2, j))]

    barrier = pltpu.get_barrier_semaphore()
    for present, device in greeted:

        @pl.when(present)
        def _():
            pl.semaphore_signal(barrier, inc=1, device_id=device, device_id_type=MESH)

    expected = functools.reduce(
        lambda a, b: a + b, [present.astype(jnp.int32) for present, _ in greeted]
    )

    stores = [
        pltpu.make_async_copy(src, dst, store_sem.at[k])
        for k, (src, dst) in enumerate(
            [
                (s_ref, s_out),
                (free.at[STEPS - 1, 1 : cx - 1], p_out.at[1 : cx - 1]),
                (free.at[STEPS - 1, 0], p_out.at[0]),
                (free.at[STEPS - 1, cx - 1], p_out.at[cx - 1]),
            ]
        )
    ]
    loads = [
        pltpu.make_async_copy(src, dst, load_sem.at[k])
        for k, (src, dst) in enumerate(
            [
                (s_hbm, s_ref),
                (p_hbm, pressure.at[0, 1 : cx + 1]),
                (q_hbm, q_ref),
                (cell_hbm, cell_ref),
                (partner_hbm, partner_ref),
                (material_hbm, material_ref),
                (input_hbm, input_ref),
                (output_hbm, output_ref),
                (transition_hbm, transition_ref),
            ]
        )
    ]
    for load in loads:
        load.start()

    def remote(src, dst, send, recv, device):
        return pltpu.make_async_remote_copy(
            src_ref=src, dst_ref=dst, send_sem=send, recv_sem=recv, device_id=device, device_id_type=MESH
        )

    def piece(c):
        return pl.ds(c * rows, rows)

    def sides(t):
        return (OWN, MIRROR) if t + 1 < STEPS else (OWN,)

    def cross(c):
        return remote(state.at[OWN, 0, piece(c)], state.at[MIRROR, 0, piece(c)], x_send.at[c], x_recv.at[c], mirror)

    s_goes = [[has_up, has_zp, has_zm], [has_down, has_zp, has_zm]]
    s_comes = [[has_down, has_zm, has_zp], [has_up, has_zm, has_zp]]

    def s_copy(t, side, way, c):
        source = 1 - side if way == OTHER else side
        device = [down_to if side else up_to, (i, j + 1), (i, j - 1)][way]
        return remote(
            state.at[source, t, piece(c)],
            found.at[t, side, way, piece(c)],
            s_send.at[t, side, way, c],
            s_recv.at[t, side, way, c],
            device,
        )

    def send_state(t, source, c):
        for side in sides(t):
            for way in (OTHER, BEFORE, AFTER):
                if (1 - side if way == OTHER else side) == source:
                    pl.when(s_goes[side][way])(s_copy(t, side, way, c).start)

    def v_copy(t):
        return remote(v_out.at[t], v_in.at[t], v_send.at[t], v_recv.at[t], mirror)

    about = remote(info_out, info_in, info_sem.at[0], info_sem.at[1], mirror)

    def plane_at(t, x):
        return pressure.at[0, x + 1] if t == 0 else free.at[t - 1, x]

    def p_copies(t):
        copies = []
        for (dx, dz), (present, device) in near.items():
            k = order[dx, dz]
            if dz == 0:
                src = plane_at(t, cx - 1 if dx > 0 else 0)
                dst = pressure.at[t, 0 if dx > 0 else cx + 1]
            elif dx == 0:
                src = face_z.at[t, 1 if dz > 0 else 0]
                dst = halo_z.at[t, 0 if dz > 0 else 1]
            else:
                src = face_c.at[t, corner_of[dx, dz]]
                dst = halo_c.at[t, corner_of[-dx, -dz]]
            copies.append(
                (present, near[-dx, -dz][0], remote(src, dst, p_send.at[t, k], p_recv.at[t, k], device))
            )
        return copies

    def send_faces(t):
        for x in range(cx):
            here = plane_at(t, x)
            face_z[t, 0, x : x + 1, :] = here[0:1, :]
            face_z[t, 1, x : x + 1, :] = here[cz - 1 : cz, :]
        for (dx, dz), k in corner_of.items():
            here = plane_at(t, cx - 1 if dx > 0 else 0)
            z = cz - 1 if dz > 0 else 0
            face_c[t, k] = here[z : z + 1, :]
        for goes, _, copy in p_copies(t):
            pl.when(goes)(copy.start)

    def e_copies(t):
        copies = []
        for (dx, dz), (present, device) in near.items():
            k = order[dx, dz]
            copy = remote(
                edge_out.at[t],
                edge_in.at[t, order[-dx, -dz]],
                e_send.at[t, k],
                e_recv.at[t, k],
                device,
            )
            copies.append((present, near[-dx, -dz][0], copy))
        return copies

    def send_edges(t, row):
        edge_out[t] = row
        for goes, _, copy in e_copies(t):
            pl.when(goes)(copy.start)

    for side in (OWN, MIRROR):
        for way, present in enumerate(s_comes[side]):

            @pl.when(jnp.logical_not(present))
            def _():
                for t in range(STEPS - side):
                    found[t, side, way] = jnp.zeros((filt, slots), jnp.float32)

    for (dx, dz), (present, _) in near.items():

        @pl.when(jnp.logical_not(present))
        def _():
            for t in range(STEPS):
                edge_in[t, order[dx, dz]] = jnp.zeros((1, slots), jnp.float32)
                if dz == 0:
                    pressure[t, 0 if dx < 0 else cx + 1] = jnp.zeros((cz, ny), jnp.float32)
                elif dx == 0:
                    halo_z[t, 0 if dz < 0 else 1] = jnp.zeros((cx, ny), jnp.float32)
                else:
                    halo_c[t, corner_of[dx, dz]] = jnp.zeros((1, ny), jnp.float32)

    live = (lax.broadcasted_iota(jnp.int32, (1, slots), 1) < count_ref[0, 0]).astype(jnp.float32)
    loads[0].wait()
    state[OWN, 0] = jnp.transpose(s_ref[...]) * live
    pl.semaphore_wait(barrier, expected)
    def send_own():
        for c in range(CHUNKS):
            send_state(0, OWN, c)

    if SEND_ORDER == 2:
        loads[1].wait()
        send_faces(0)
    for c in range(CHUNKS):
        cross(c).start()
    if SEND_ORDER == 0:
        send_own()
    if SEND_ORDER <= 1:
        loads[1].wait()
        send_faces(0)
    if SEND_ORDER == 1:
        send_own()
    for k, load in enumerate(loads):
        if k > 1:
            load.wait()
    info_out[...] = jnp.concatenate(
        [
            partner_ref[...].astype(jnp.float32),
            material_ref[...].astype(jnp.float32),
            live,
            jnp.zeros((5, slots), jnp.float32),
        ],
        axis=0,
    )
    about.start()

    along = lax.rem(cell_ref[...], ny).astype(jnp.float32)
    column[...] = jnp.transpose(jnp.broadcast_to(along, (lanes, slots)))
    send_edges(0, along)
    lane = lax.broadcasted_iota(jnp.int32, (cz, lanes), 1).astype(jnp.float32)
    for x in range(cx):
        for part in range(parts):
            mask[x, :, part * lanes : (part + 1) * lanes] = (
                column[x * cz : (x + 1) * cz] == lane + float(part * lanes)
            ).astype(jnp.float32)

    in_t = jnp.transpose(jnp.concatenate([input_ref[...], output_ref[...]], axis=0))
    slot_down = lax.broadcasted_iota(jnp.int32, (slots, slots), 0).astype(jnp.float32)

    def describe(side, partner, material):
        low_x, high_x = 1.0, 2.0
        is_upper = (upper if side == OWN else 1 - upper).astype(jnp.float32)
        for d, code in enumerate([0.0, high_x - is_upper, low_x + is_upper, 3.0, 4.0]):
            gather[side, d] = (slot_down + code * slots == partner).astype(jnp.float32).astype(jnp.bfloat16)
        for m in range(kinds):
            kind[side, m] = (material == float(m)).astype(jnp.float32)
        for target, first in ((drive, 0), (readout, kinds)):
            target[side] = functools.reduce(
                lambda a, b: a + b, [in_t[:, first + m : first + m + 1] * kind[side, m] for m in range(kinds)]
            )

    describe(OWN, partner_ref[...].astype(jnp.float32), material_ref[...].astype(jnp.float32))
    for m in range(kinds):
        high, low = split(jnp.transpose(transition_ref[m]))
        here = slice(m * filt, (m + 1) * filt)
        mix_a[here, 0:filt] = high
        mix_a[here, filt : 2 * filt] = high
        mix_b[here, :] = low

    def pick(x, change):
        chosen = mask[x] * change
        picked[pl.ds(x * cz, cz), :] = functools.reduce(
            lambda a, b: a + b, [chosen[:, k * lanes : (k + 1) * lanes] for k in range(parts)]
        )

    def picked_row():
        return jnp.sum(jnp.transpose(picked[...]), axis=0, keepdims=True)

    def first_change(x, _):
        pick(x, pressure[0, x + 1] - q_ref[x])
        return 0

    lax.fori_loop(0, cx, first_change, 0, unroll=4)
    velocity = [picked_row(), None]
    v_out[0] = velocity[OWN]
    v_copy(0).start()

    iota_z = lax.broadcasted_iota(jnp.int32, (cz, ny), 0)
    iota_y = lax.broadcasted_iota(jnp.int32, (cz, ny), 1)
    rest_w = face_w - edge_w

    def both_y(value):
        return jnp.where(iota_y == 0, 0.0, pltpu.roll(value, 1, 1)) + jnp.where(
            iota_y == ny - 1, 0.0, pltpu.roll(value, ny - 1, 1)
        )

    def both_z(here, low, high):
        return jnp.where(iota_z == 0, low, pltpu.roll(here, 1, 0)) + jnp.where(
            iota_z == cz - 1, high, pltpu.roll(here, cz - 1, 0)
        )

    def turn_edges(t, slot, ways):
        none = jnp.zeros((1, slots), jnp.float32)
        rows_in = [edge_in[t, k] if way in ways else none for way, k in order.items()]
        turned[slot, :, 0:8] = jnp.transpose(jnp.concatenate(rows_in, axis=0))

    def spread(way):
        (dx, dz), k = way, order[way]
        x, z = (0 if dx > 0 else cx - 1), (0 if dz > 0 else cz - 1)
        if dz == 0:
            at = pl.ds(x * cz, cz)
        elif dx == 0:
            at = pl.ds(z, cx, cz)
        else:
            at = pl.ds(x * cz + z, 1)
        place, value = turned[0, at, :][:, k : k + 1], turned[2 if dx else 1, at, :][:, k : k + 1]
        along_y = lax.broadcasted_iota(jnp.int32, (place.shape[0], ny), 1).astype(jnp.float32)
        return jnp.where(place == along_y, value, 0.0)

    along_z = [way for way in order if way[0] == 0]
    along_x = [way for way in order if way[0] != 0]

    def wait_for(t, ways):
        copies = p_copies(t)
        if t > 0:
            copies += e_copies(t)
        for n, (_, comes, copy) in enumerate(copies):
            if list(order)[n % 8] in ways:
                pl.when(comes)(copy.wait_recv)

    def pressure_free(t):
        last = t + 1 == STEPS

        def inside(x):
            return both_z(pressure[t, x + 1], halo_z[t, 0, pl.ds(x, 1), :], halo_z[t, 1, pl.ds(x, 1), :])

        def one(x, before, here, after):
            left, mid, right = pressure[t, x], pressure[t, x + 1], pressure[t, x + 2]
            past = q_ref[x] if t == 0 else pressure[t - 1, x + 1]
            beside = left + right
            even = edge_w * ((beside + mid) + (before + here + after))
            total = both_y(even + rest_w * mid) + even + rest_w * (here + beside) + (centre_w - edge_w) * mid
            value = 2.0 * mid - past + courant * total
            if last:
                free[t, x] = value - column[pl.ds(x * cz, cz), 0:1] * mask[x]
            else:
                free[t, x] = value
                pick(x, value - mid)

        def step(x, held):
            before, here = held
            after = inside(x + 1)
            one(x, before, here, after)
            return here, after

        if t == 1:
            for _, comes, copy in e_copies(0):
                pl.when(comes)(copy.wait_recv)
            turn_edges(0, 0, list(order))
        wait_for(t, along_z)
        if t > 0:
            turn_edges(t, 1, along_z)
            for end in (0, 1):
                halo_z[t, end] -= spread((0, 2 * end - 1))
        before, here = lax.fori_loop(1, cx - 1, step, (inside(0), inside(1)), unroll=2)
        if last:
            stores[1].start()
        wait_for(t, along_x)
        if t > 0:
            turn_edges(t, 2, along_x)
            for end in (0, 1):
                side = 2 * end - 1
                pressure[t, end * (cx + 1)] -= spread((side, 0))
                for z in (-1, 1):
                    halo_c[t, corner_of[side, z]] -= spread((side, z))

        def ends(end):
            at = [halo_c[t, corner_of[2 * end - 1, z]] for z in (-1, 1)]
            return both_z(pressure[t, end * (cx + 1)], *at)

        one(cx - 1, before, here, ends(1))
        one(0, ends(0), inside(0), inside(1))
        if last:
            stores[2].start()
            stores[3].start()
            return None
        return picked_row()

    def gathered(side, d, value):
        high, low = split(value)
        got = dot(jnp.concatenate([high, low], axis=0), gather[side, d])
        return got[: value.shape[0]] + got[value.shape[0] :]

    def mixed(side, t):
        now = state[side, t]
        high, low = split(now)
        stacked = jnp.concatenate([high, low], axis=0)
        moved = dot(mix_a[...], stacked) + dot(mix_b[...], high)
        total = functools.reduce(
            lambda a, b: a + b, [moved[m * filt : (m + 1) * filt] * kind[side, m] for m in range(kinds)]
        )
        own = dot(stacked, gather[side, 0])
        base[side] = total + coupling * (own[:filt] + own[filt:] - now)

    def across(side, t):
        base[side] += velocity[side] * drive[side] + coupling * gathered(side, 1, state[1 - side, t])

    def do_pressure(t):
        change = pressure_free(t)
        if t + 1 == STEPS:
            return None
        if t + 2 < STEPS:
            v_out[t + 1] = change
            v_copy(t + 1).start()
        send_faces(t + 1)
        return change

    def come(side, t):
        for c in range(CHUNKS):
            total = base[side, piece(c)]
            for way in (OTHER, BEFORE, AFTER):
                pl.when(s_comes[side][way])(s_copy(t, side, way, c).wait_recv)
                total = total + coupling * gathered(side, way + 2, found[t, side, way, piece(c)])
            state[side, t + 1, piece(c)] = total * lives[side]
            if t + 1 < STEPS and (c + 1 < CHUNKS or side == MIRROR):
                send_state(t + 1, side, c)

    if SEND_ORDER == 2:
        send_own()
    mixed(OWN, 0)
    for c in range(CHUNKS):
        cross(c).wait_recv()
        send_state(0, MIRROR, c)
    about.wait_recv()
    describe(MIRROR, info_in[0:1, :], info_in[1:2, :])
    lives = [live, info_in[2:3, :]]

    for t in range(STEPS):
        if t > 0:
            mixed(OWN, t)
        across(OWN, t)
        if PRESSURE_AT[t] == 0:
            change = do_pressure(t)
        come(OWN, t)
        product = state[OWN, t + 1] * readout[OWN]
        if t + 1 < STEPS:
            correction = jnp.sum(product, axis=0, keepdims=True)
            send_edges(t + 1, correction)
            send_state(t + 1, OWN, CHUNKS - 1)
        else:
            s_ref[...] = jnp.transpose(state[OWN, STEPS])
            stores[0].start()
        column[...] = jnp.broadcast_to(jnp.sum(jnp.transpose(product), axis=1, keepdims=True), (slots, lanes))
        if PRESSURE_AT[t] == 1:
            change = do_pressure(t)
        if t + 1 < STEPS:
            mixed(MIRROR, t)
            v_copy(t).wait_recv()
            velocity[MIRROR] = v_in[t] - (behind if t > 0 else 0.0)
            across(MIRROR, t)
            come(MIRROR, t)
            behind = jnp.sum(state[MIRROR, t + 1] * readout[MIRROR], axis=0, keepdims=True)
            if PRESSURE_AT[t] == 2:
                change = do_pressure(t)
            velocity[OWN] = change - correction
            for x in range(cx):
                pressure[t + 1, x + 1] = free[t, x] - column[x * cz : (x + 1) * cz, 0:1] * mask[x]

    for store in stores:
        store.wait()
    about.wait_send()
    for c in range(CHUNKS):
        cross(c).wait_send()
    for t in range(STEPS - 1):
        v_copy(t).wait_send()
    for t in range(STEPS):
        for side in sides(t):
            for way, goes in enumerate(s_goes[side]):

                @pl.when(goes)
                def _():
                    for c in range(CHUNKS):
                        s_copy(t, side, way, c).wait_send()

        for goes, _, copy in p_copies(t) + e_copies(t):
            pl.when(goes)(copy.wait_send)


def hand_over(p_ref, s_ref, p_out, s_out, p_held, s_held, load_sem, store_sem):
    part = p_ref.shape[0] // 4
    pieces = [(s_ref, s_held, s_out)] + [
        (p_ref.at[here], p_held.at[here], p_out.at[here]) for here in [pl.ds(k * part, part) for k in range(4)]
    ]
    loads = [pltpu.make_async_copy(src, held, load_sem.at[k]) for k, (src, held, _) in enumerate(pieces)]
    stores = [pltpu.make_async_copy(held, dst, store_sem.at[k]) for k, (_, held, dst) in enumerate(pieces)]
    for load in loads:
        load.start()
    for load, store in zip(loads, stores):
        load.wait()
        store.start()
    for store in stores:
        store.wait()


def per_device(
    pressure,
    previous,
    states,
    wall_cell,
    wall_count,
    material,
    partner,
    transitions,
    inputs,
    outputs,
):
    cx, cz, ny = pressure.shape
    slots, filt = states.shape[2:]
    kinds = transitions.shape[0]
    sizes = (lax.axis_size("gx"), lax.axis_size("gz"))
    f32, bf16 = jnp.float32, jnp.bfloat16
    vmem = pl.BlockSpec(memory_space=pltpu.VMEM)
    smem = pl.BlockSpec(memory_space=pltpu.SMEM)
    hbm = pl.BlockSpec(memory_space=pltpu.HBM)
    pressure_out, states_out = pl.pallas_call(
        functools.partial(kernel, sizes),
        out_shape=[
            jax.ShapeDtypeStruct((cx, cz, ny), f32),
            jax.ShapeDtypeStruct((slots, filt), f32),
        ],
        in_specs=[hbm, hbm, hbm, hbm, smem, hbm, hbm, hbm, hbm, hbm],
        out_specs=[hbm, hbm],
        scratch_shapes=[
            pltpu.VMEM((cx, cz, ny), f32),
            pltpu.VMEM((slots, filt), f32),
            pltpu.VMEM((1, slots), jnp.int32),
            pltpu.VMEM((1, slots), jnp.int32),
            pltpu.VMEM((1, slots), jnp.int32),
            pltpu.VMEM((kinds, filt, filt), f32),
            pltpu.VMEM((kinds, filt), f32),
            pltpu.VMEM((kinds, filt), f32),
            pltpu.VMEM((2, STEPS + 1, filt, slots), f32),
            pltpu.VMEM((STEPS, 2, 3, filt, slots), f32),
            pltpu.VMEM((2, filt, slots), f32),
            pltpu.VMEM((8, slots), f32),
            pltpu.VMEM((8, slots), f32),
            pltpu.VMEM((STEPS - 1, 1, slots), f32),
            pltpu.VMEM((STEPS - 1, 1, slots), f32),
            pltpu.VMEM((2, kinds, 1, slots), f32),
            pltpu.VMEM((2, 5, slots, slots), bf16),
            pltpu.VMEM((kinds * filt, 2 * filt), bf16),
            pltpu.VMEM((kinds * filt, filt), bf16),
            pltpu.VMEM((2, filt, slots), f32),
            pltpu.VMEM((2, filt, slots), f32),
            pltpu.VMEM((cx, cz, ny), f32),
            pltpu.VMEM((STEPS, cx + 2, cz, ny), f32),
            pltpu.VMEM((STEPS, 2, cx, ny), f32),
            pltpu.VMEM((STEPS, 4, 1, ny), f32),
            pltpu.VMEM((STEPS, 2, cx, ny), f32),
            pltpu.VMEM((STEPS, 4, 1, ny), f32),
            pltpu.VMEM((STEPS, 1, slots), f32),
            pltpu.VMEM((STEPS, 8, 1, slots), f32),
            pltpu.VMEM((3, slots, 128), f32),
            pltpu.VMEM((slots, 128), f32),
            pltpu.VMEM((STEPS, cx, cz, ny), f32),
            pltpu.VMEM((slots, 128), f32),
            pltpu.SemaphoreType.DMA((9,)),
            pltpu.SemaphoreType.DMA((4,)),
            pltpu.SemaphoreType.DMA((2,)),
            pltpu.SemaphoreType.DMA((CHUNKS,)),
            pltpu.SemaphoreType.DMA((CHUNKS,)),
            pltpu.SemaphoreType.DMA((STEPS - 1,)),
            pltpu.SemaphoreType.DMA((STEPS - 1,)),
            pltpu.SemaphoreType.DMA((STEPS, 2, 3, CHUNKS)),
            pltpu.SemaphoreType.DMA((STEPS, 2, 3, CHUNKS)),
            pltpu.SemaphoreType.DMA((STEPS, 8)),
            pltpu.SemaphoreType.DMA((STEPS, 8)),
            pltpu.SemaphoreType.DMA((STEPS, 8)),
            pltpu.SemaphoreType.DMA((STEPS, 8)),
        ],
        compiler_params=pltpu.CompilerParams(
            collective_id=0, has_side_effects=True, vmem_limit_bytes=60 * 1024 * 1024
        ),
        name="leapfrog",
    )(
        pressure,
        previous,
        states.reshape(slots, filt),
        wall_cell.reshape(1, slots),
        wall_count,
        material.reshape(1, slots),
        partner.reshape(1, slots),
        transitions,
        inputs,
        outputs,
    )
    pressure_out, states_out = pl.pallas_call(
        hand_over,
        out_shape=[
            jax.ShapeDtypeStruct((cx, cz, ny), f32),
            jax.ShapeDtypeStruct((slots, filt), f32),
        ],
        in_specs=[hbm, hbm],
        out_specs=[hbm, hbm],
        scratch_shapes=[
            pltpu.VMEM((cx, cz, ny), f32),
            pltpu.VMEM((slots, filt), f32),
            pltpu.SemaphoreType.DMA((5,)),
            pltpu.SemaphoreType.DMA((5,)),
        ],
        name="hand_over",
    )(pressure_out, states_out)
    return pressure_out, states_out.reshape(1, 1, slots, filt)


def solution(mesh):
    placed = (
        P("gx", "gz", None),
        P("gx", "gz", None),
        P("gx", "gz", None, None),
        P("gx", "gz", None),
        P("gx", "gz"),
        P("gx", "gz", None),
        P("gx", "gz", None),
        P(),
        P(),
        P(),
    )
    return jax.shard_map(
        per_device,
        mesh=mesh,
        in_specs=placed,
        out_specs=(P("gx", "gz", None), P("gx", "gz", None, None)),
        check_vma=False,
    )
```

```python
import functools

import jax
import jax.numpy as jnp
from jax import lax
from jax.experimental import pallas as pl
from jax.experimental.pallas import tpu as pltpu
from jax.sharding import PartitionSpec as P

MESH = pl.DeviceIdType.MESH
STEPS = 3
CHUNKS = 2
PRESSURE_AT = (1, 1, 1)
OTHER, BEFORE, AFTER = range(3)
OWN, MIRROR = range(2)

face_w = 0.5
edge_w = 0.0625
corner_w = 0.0625
centre_w = -(6 * face_w + 12 * edge_w + 8 * corner_w)
courant = 0.3
coupling = 0.3


def split(value):
    high = value.astype(jnp.bfloat16)
    low = (value - high.astype(jnp.float32)).astype(jnp.bfloat16)
    return high, low


def dot(left, right):
    return jnp.dot(left, right, preferred_element_type=jnp.float32)


def kernel(
    sizes,
    p_hbm,
    q_hbm,
    s_hbm,
    cell_hbm,
    count_ref,
    material_hbm,
    partner_hbm,
    transition_hbm,
    input_hbm,
    output_hbm,
    p_out,
    s_out,
    q_ref,
    s_ref,
    cell_ref,
    material_ref,
    partner_ref,
    transition_ref,
    input_ref,
    output_ref,
    state,
    found,
    base,
    info_out,
    info_in,
    v_out,
    v_in,
    kind,
    gather,
    mix_a,
    mix_b,
    drive,
    readout,
    mask,
    pressure,
    halo_z,
    halo_c,
    face_z,
    face_c,
    edge_out,
    edge_in,
    turned,
    column,
    free,
    picked,
    load_sem,
    store_sem,
    info_sem,
    x_send,
    x_recv,
    v_send,
    v_recv,
    s_send,
    s_recv,
    p_send,
    p_recv,
    e_send,
    e_recv,
):
    n_gx, n_gz = sizes
    cx, cz, ny = q_ref.shape
    slots, filt = s_ref.shape
    kinds = transition_ref.shape[0]
    rows = filt // CHUNKS
    lanes = 128
    parts = ny // lanes
    i, j = lax.axis_index("gx"), lax.axis_index("gz")
    upper = lax.rem(i, 2)
    has_xm, has_xp = i > 0, i < n_gx - 1
    has_zm, has_zp = j > 0, j < n_gz - 1
    mirror = (i + 1 - 2 * upper, j)
    up_to, down_to = (i + 2 - 4 * upper, j), (i - 2 + 4 * upper, j)
    has_up = jnp.logical_and(up_to[0] >= 0, up_to[0] < n_gx)
    has_down = jnp.logical_and(down_to[0] >= 0, down_to[0] < n_gx)

    near = {}
    for dx in (-1, 0, 1):
        for dz in (-1, 0, 1):
            if dx or dz:
                present = [has_xm, None, has_xp][dx + 1], [has_zm, None, has_zp][dz + 1]
                present = [one for one in present if one is not None]
                near[dx, dz] = (functools.reduce(jnp.logical_and, present), (i + dx, j + dz))
    order = {way: k for k, way in enumerate(near)}
    corner_of = {(-1, -1): 0, (-1, 1): 1, (1, -1): 2, (1, 1): 3}
    greeted = list(near.values()) + [(i >= 2, (i - 2, j)), (i < n_gx - 2, (i + 2, j))]

    barrier = pltpu.get_barrier_semaphore()
    for present, device in greeted:

        @pl.when(present)
        def _():
            pl.semaphore_signal(barrier, inc=1, device_id=device, device_id_type=MESH)

    expected = functools.reduce(
        lambda a, b: a + b, [present.astype(jnp.int32) for present, _ in greeted]
    )

    stores = [
        pltpu.make_async_copy(src, dst, store_sem.at[k])
        for k, (src, dst) in enumerate(
            [
                (s_ref, s_out),
                (free.at[STEPS - 1, 1 : cx - 1], p_out.at[1 : cx - 1]),
                (free.at[STEPS - 1, 0], p_out.at[0]),
                (free.at[STEPS - 1, cx - 1], p_out.at[cx - 1]),
            ]
        )
    ]
    loads = [
        pltpu.make_async_copy(src, dst, load_sem.at[k])
        for k, (src, dst) in enumerate(
            [
                (s_hbm, s_ref),
                (p_hbm, pressure.at[0, 1 : cx + 1]),
                (q_hbm, q_ref),
                (cell_hbm, cell_ref),
                (partner_hbm, partner_ref),
                (material_hbm, material_ref),
                (input_hbm, input_ref),
                (output_hbm, output_ref),
                (transition_hbm, transition_ref),
            ]
        )
    ]
    for load in loads:
        load.start()

    def remote(src, dst, send, recv, device):
        return pltpu.make_async_remote_copy(
            src_ref=src, dst_ref=dst, send_sem=send, recv_sem=recv, device_id=device, device_id_type=MESH
        )

    def piece(c):
        return pl.ds(c * rows, rows)

    def sides(t):
        return (OWN, MIRROR) if t + 1 < STEPS else (OWN,)

    def cross(c):
        return remote(state.at[OWN, 0, piece(c)], state.at[MIRROR, 0, piece(c)], x_send.at[c], x_recv.at[c], mirror)

    s_goes = [[has_up, has_zp, has_zm], [has_down, has_zp, has_zm]]
    s_comes = [[has_down, has_zm, has_zp], [has_up, has_zm, has_zp]]

    def s_copy(t, side, way, c):
        source = 1 - side if way == OTHER else side
        device = [down_to if side else up_to, (i, j + 1), (i, j - 1)][way]
        return remote(
            state.at[source, t, piece(c)],
            found.at[t, side, way, piece(c)],
            s_send.at[t, side, way, c],
            s_recv.at[t, side, way, c],
            device,
        )

    def send_state(t, source, c):
        for side in sides(t):
            for way in (OTHER, BEFORE, AFTER):
                if (1 - side if way == OTHER else side) == source:
                    pl.when(s_goes[side][way])(s_copy(t, side, way, c).start)

    def v_copy(t):
        return remote(v_out.at[t], v_in.at[t], v_send.at[t], v_recv.at[t], mirror)

    about = remote(info_out, info_in, info_sem.at[0], info_sem.at[1], mirror)

    def plane_at(t, x):
        return pressure.at[0, x + 1] if t == 0 else free.at[t - 1, x]

    def p_copies(t, ways=None):
        copies = []
        for (dx, dz), (present, device) in near.items():
            if ways is not None and (-dx, -dz) not in ways:
                continue
            k = order[dx, dz]
            if dz == 0:
                src = plane_at(t, cx - 1 if dx > 0 else 0)
                dst = pressure.at[t, 0 if dx > 0 else cx + 1]
            elif dx == 0:
                src = face_z.at[t, 1 if dz > 0 else 0]
                dst = halo_z.at[t, 0 if dz > 0 else 1]
            else:
                src = face_c.at[t, corner_of[dx, dz]]
                dst = halo_c.at[t, corner_of[-dx, -dz]]
            copies.append(
                (present, near[-dx, -dz][0], remote(src, dst, p_send.at[t, k], p_recv.at[t, k], device))
            )
        return copies

    along_z = [way for way in order if way[0] == 0]
    along_x = [way for way in order if way[0] != 0]

    def send_faces(t, ways):
        if ways == along_z:
            for x in range(cx):
                here = plane_at(t, x)
                face_z[t, 0, x : x + 1, :] = here[0:1, :]
                face_z[t, 1, x : x + 1, :] = here[cz - 1 : cz, :]
        else:
            for (dx, dz), k in corner_of.items():
                here = plane_at(t, cx - 1 if dx > 0 else 0)
                z = cz - 1 if dz > 0 else 0
                face_c[t, k] = here[z : z + 1, :]
        for goes, _, copy in p_copies(t, ways):
            pl.when(goes)(copy.start)

    def e_copies(t, ways=None):
        copies = []
        for (dx, dz), (present, device) in near.items():
            if ways is not None and (-dx, -dz) not in ways:
                continue
            k = order[dx, dz]
            copy = remote(
                edge_out.at[t],
                edge_in.at[t, order[-dx, -dz]],
                e_send.at[t, k],
                e_recv.at[t, k],
                device,
            )
            copies.append((present, near[-dx, -dz][0], copy))
        return copies

    def send_edges(t, row):
        edge_out[t] = row
        for goes, _, copy in e_copies(t):
            pl.when(goes)(copy.start)

    for side in (OWN, MIRROR):
        for way, present in enumerate(s_comes[side]):

            @pl.when(jnp.logical_not(present))
            def _():
                for t in range(STEPS - side):
                    found[t, side, way] = jnp.zeros((filt, slots), jnp.float32)

    for (dx, dz), (present, _) in near.items():

        @pl.when(jnp.logical_not(present))
        def _():
            for t in range(STEPS):
                edge_in[t, order[dx, dz]] = jnp.zeros((1, slots), jnp.float32)
                if dz == 0:
                    pressure[t, 0 if dx < 0 else cx + 1] = jnp.zeros((cz, ny), jnp.float32)
                elif dx == 0:
                    halo_z[t, 0 if dz < 0 else 1] = jnp.zeros((cx, ny), jnp.float32)
                else:
                    halo_c[t, corner_of[dx, dz]] = jnp.zeros((1, ny), jnp.float32)

    live = (lax.broadcasted_iota(jnp.int32, (1, slots), 1) < count_ref[0, 0]).astype(jnp.float32)
    loads[0].wait()
    state[OWN, 0] = jnp.transpose(s_ref[...]) * live
    pl.semaphore_wait(barrier, expected)
    def send_own():
        for c in range(CHUNKS):
            send_state(0, OWN, c)

    loads[1].wait()
    send_faces(0, along_x)
    send_faces(0, along_z)
    for c in range(CHUNKS):
        cross(c).start()
    for k, load in enumerate(loads):
        if k > 1:
            load.wait()
    info_out[...] = jnp.concatenate(
        [
            partner_ref[...].astype(jnp.float32),
            material_ref[...].astype(jnp.float32),
            live,
            jnp.zeros((5, slots), jnp.float32),
        ],
        axis=0,
    )
    about.start()

    along = lax.rem(cell_ref[...], ny).astype(jnp.float32)
    column[0] = jnp.transpose(jnp.broadcast_to(along, (lanes, slots)))
    send_edges(0, along)
    lane = lax.broadcasted_iota(jnp.int32, (cz, lanes), 1).astype(jnp.float32)
    for x in range(cx):
        for part in range(parts):
            mask[x, :, part * lanes : (part + 1) * lanes] = (
                column[0, x * cz : (x + 1) * cz] == lane + float(part * lanes)
            ).astype(jnp.float32)

    in_t = jnp.transpose(jnp.concatenate([input_ref[...], output_ref[...]], axis=0))
    slot_down = lax.broadcasted_iota(jnp.int32, (slots, slots), 0).astype(jnp.float32)

    def describe(side, partner, material):
        low_x, high_x = 1.0, 2.0
        is_upper = (upper if side == OWN else 1 - upper).astype(jnp.float32)
        for d, code in enumerate([0.0, high_x - is_upper, low_x + is_upper, 3.0, 4.0]):
            gather[side, d] = (slot_down + code * slots == partner).astype(jnp.float32).astype(jnp.bfloat16)
        for m in range(kinds):
            kind[side, m] = (material == float(m)).astype(jnp.float32)
        for target, first in ((drive, 0), (readout, kinds)):
            target[side] = functools.reduce(
                lambda a, b: a + b, [in_t[:, first + m : first + m + 1] * kind[side, m] for m in range(kinds)]
            )

    describe(OWN, partner_ref[...].astype(jnp.float32), material_ref[...].astype(jnp.float32))
    for m in range(kinds):
        high, low = split(jnp.transpose(transition_ref[m]))
        here = slice(m * filt, (m + 1) * filt)
        mix_a[here, 0:filt] = high
        mix_a[here, filt : 2 * filt] = high
        mix_b[here, :] = low

    def pick(x, change):
        chosen = mask[x] * change
        picked[pl.ds(x * cz, cz), :] = functools.reduce(
            lambda a, b: a + b, [chosen[:, k * lanes : (k + 1) * lanes] for k in range(parts)]
        )

    def picked_row():
        return jnp.sum(jnp.transpose(picked[...]), axis=0, keepdims=True)

    def first_change(x, _):
        pick(x, pressure[0, x + 1] - q_ref[x])
        return 0

    lax.fori_loop(0, cx, first_change, 0, unroll=4)
    velocity = [picked_row(), None]
    v_out[0] = velocity[OWN]
    v_copy(0).start()

    iota_z = lax.broadcasted_iota(jnp.int32, (cz, ny), 0)
    iota_y = lax.broadcasted_iota(jnp.int32, (cz, ny), 1)
    rest_w = face_w - edge_w

    def both_y(value):
        return jnp.where(iota_y == 0, 0.0, pltpu.roll(value, 1, 1)) + jnp.where(
            iota_y == ny - 1, 0.0, pltpu.roll(value, ny - 1, 1)
        )

    def both_z(here, low, high):
        return jnp.where(iota_z == 0, low, pltpu.roll(here, 1, 0)) + jnp.where(
            iota_z == cz - 1, high, pltpu.roll(here, cz - 1, 0)
        )

    def turn_edges(t, slot, ways):
        none = jnp.zeros((1, slots), jnp.float32)
        rows_in = [edge_in[t, k] if way in ways else none for way, k in order.items()]
        turned[slot, :, 0:8] = jnp.transpose(jnp.concatenate(rows_in, axis=0))

    def spread(way):
        (dx, dz), k = way, order[way]
        x, z = (0 if dx > 0 else cx - 1), (0 if dz > 0 else cz - 1)
        if dz == 0:
            at = pl.ds(x * cz, cz)
        elif dx == 0:
            at = pl.ds(z, cx, cz)
        else:
            at = pl.ds(x * cz + z, 1)
        place, value = turned[0, at, :][:, k : k + 1], turned[2 if dx else 1, at, :][:, k : k + 1]
        along_y = lax.broadcasted_iota(jnp.int32, (place.shape[0], ny), 1).astype(jnp.float32)
        return jnp.where(place == along_y, value, 0.0)

    def wait_for(t, ways):
        for _, comes, copy in p_copies(t, ways) + (e_copies(t, ways) if t > 0 else []):
            pl.when(comes)(copy.wait_recv)

    def pressure_free(t):
        last = t + 1 == STEPS
        if t > 0:
            for x in range(cx):
                pressure[t, x + 1] = free[t - 1, x] - column[t - 1, x * cz : (x + 1) * cz, 0:1] * mask[x]

        def inside(x):
            return both_z(pressure[t, x + 1], halo_z[t, 0, pl.ds(x, 1), :], halo_z[t, 1, pl.ds(x, 1), :])

        def one(x, before, here, after):
            left, mid, right = pressure[t, x], pressure[t, x + 1], pressure[t, x + 2]
            past = q_ref[x] if t == 0 else pressure[t - 1, x + 1]
            beside = left + right
            even = edge_w * ((beside + mid) + (before + here + after))
            total = both_y(even + rest_w * mid) + even + rest_w * (here + beside) + (centre_w - edge_w) * mid
            value = 2.0 * mid - past + courant * total
            if last:
                free[t, x] = value - column[t, pl.ds(x * cz, cz), 0:1] * mask[x]
            else:
                free[t, x] = value
                pick(x, value - mid)

        def step(x, held):
            before, here = held
            after = inside(x + 1)
            one(x, before, here, after)
            return here, after

        if t == 1:
            for _, comes, copy in e_copies(0):
                pl.when(comes)(copy.wait_recv)
            turn_edges(0, 0, list(order))
        wait_for(t, along_z)
        if t > 0:
            turn_edges(t, 1, along_z)
            for end in (0, 1):
                halo_z[t, end] -= spread((0, 2 * end - 1))
        def inner():
            lax.fori_loop(1, cx - 1, step, (inside(0), inside(1)), unroll=2)

        def outer():
            wait_for(t, along_x)
            if t > 0:
                turn_edges(t, 2, along_x)
                for end in (0, 1):
                    side = 2 * end - 1
                    pressure[t, end * (cx + 1)] -= spread((side, 0))
                    for z in (-1, 1):
                        halo_c[t, corner_of[side, z]] -= spread((side, z))
            ends = []
            for end in (0, 1):
                at = [halo_c[t, corner_of[2 * end - 1, z]] for z in (-1, 1)]
                ends.append(both_z(pressure[t, end * (cx + 1)], *at))
            one(0, ends[0], inside(0), inside(1))
            one(cx - 1, inside(cx - 2), inside(cx - 1), ends[1])

        if last:
            inner()
            stores[1].start()
            outer()
            stores[2].start()
            stores[3].start()
            return None
        outer()
        send_faces(t + 1, along_x)
        inner()
        send_faces(t + 1, along_z)
        return picked_row()

    def gathered(side, d, value):
        high, low = split(value)
        got = dot(jnp.concatenate([high, low], axis=0), gather[side, d])
        return got[: value.shape[0]] + got[value.shape[0] :]

    def mixed(side, t):
        now = state[side, t]
        high, low = split(now)
        stacked = jnp.concatenate([high, low], axis=0)
        moved = dot(mix_a[...], stacked) + dot(mix_b[...], high)
        total = functools.reduce(
            lambda a, b: a + b, [moved[m * filt : (m + 1) * filt] * kind[side, m] for m in range(kinds)]
        )
        own = dot(stacked, gather[side, 0])
        base[side] = total + coupling * (own[:filt] + own[filt:] - now)

    def across(side, t):
        base[side] += coupling * gathered(side, 1, state[1 - side, t])

    def do_pressure(t):
        change = pressure_free(t)
        if t + 1 == STEPS:
            return None
        if t + 2 < STEPS:
            v_out[t + 1] = change
            v_copy(t + 1).start()
        return change

    def come(side, t):
        for c in range(CHUNKS):
            total = base[side, piece(c)]
            for way in (OTHER, BEFORE, AFTER):
                pl.when(s_comes[side][way])(s_copy(t, side, way, c).wait_recv)
                total = total + coupling * gathered(side, way + 2, found[t, side, way, piece(c)])
            state[side, t + 1, piece(c)] = total * lives[side]
            if t + 1 < STEPS and (c + 1 < CHUNKS or side == MIRROR):
                send_state(t + 1, side, c)

    send_own()
    mixed(OWN, 0)
    for c in range(CHUNKS):
        cross(c).wait_recv()
        send_state(0, MIRROR, c)
    about.wait_recv()
    describe(MIRROR, info_in[0:1, :], info_in[1:2, :])
    lives = [live, info_in[2:3, :]]

    for t in range(STEPS):
        if t > 0:
            mixed(OWN, t)
        across(OWN, t)
        base[OWN] += velocity[OWN] * drive[OWN]
        if t == 1:
            mixed(MIRROR, t)
            across(MIRROR, t)
        if PRESSURE_AT[t] == 0:
            change = do_pressure(t)
        come(OWN, t)
        product = state[OWN, t + 1] * readout[OWN]
        if t + 1 < STEPS:
            correction = jnp.sum(product, axis=0, keepdims=True)
            send_edges(t + 1, correction)
            send_state(t + 1, OWN, CHUNKS - 1)
        else:
            s_ref[...] = jnp.transpose(state[OWN, STEPS])
            stores[0].start()
        column[t] = jnp.broadcast_to(jnp.sum(jnp.transpose(product), axis=1, keepdims=True), (slots, lanes))
        if PRESSURE_AT[t] == 1:
            change = do_pressure(t)
        if t + 1 < STEPS:
            if t == 0:
                mixed(MIRROR, t)
                across(MIRROR, t)
            v_copy(t).wait_recv()
            base[MIRROR] += (v_in[t] - (behind if t > 0 else 0.0)) * drive[MIRROR]
            come(MIRROR, t)
            behind = jnp.sum(state[MIRROR, t + 1] * readout[MIRROR], axis=0, keepdims=True)
            if PRESSURE_AT[t] == 2:
                change = do_pressure(t)
            velocity[OWN] = change - correction

    for store in stores:
        store.wait()
    about.wait_send()
    for c in range(CHUNKS):
        cross(c).wait_send()
    for t in range(STEPS - 1):
        v_copy(t).wait_send()
    for t in range(STEPS):
        for side in sides(t):
            for way, goes in enumerate(s_goes[side]):

                @pl.when(goes)
                def _():
                    for c in range(CHUNKS):
                        s_copy(t, side, way, c).wait_send()

        for goes, _, copy in p_copies(t) + e_copies(t):
            pl.when(goes)(copy.wait_send)


def hand_over(p_ref, s_ref, p_out, s_out, p_held, s_held, load_sem, store_sem):
    part = p_ref.shape[0] // 4
    pieces = [(s_ref, s_held, s_out)] + [
        (p_ref.at[here], p_held.at[here], p_out.at[here]) for here in [pl.ds(k * part, part) for k in range(4)]
    ]
    loads = [pltpu.make_async_copy(src, held, load_sem.at[k]) for k, (src, held, _) in enumerate(pieces)]
    stores = [pltpu.make_async_copy(held, dst, store_sem.at[k]) for k, (_, held, dst) in enumerate(pieces)]
    for load in loads:
        load.start()
    for load, store in zip(loads, stores):
        load.wait()
        store.start()
    for store in stores:
        store.wait()


def per_device(
    pressure,
    previous,
    states,
    wall_cell,
    wall_count,
    material,
    partner,
    transitions,
    inputs,
    outputs,
):
    cx, cz, ny = pressure.shape
    slots, filt = states.shape[2:]
    kinds = transitions.shape[0]
    sizes = (lax.axis_size("gx"), lax.axis_size("gz"))
    f32, bf16 = jnp.float32, jnp.bfloat16
    vmem = pl.BlockSpec(memory_space=pltpu.VMEM)
    smem = pl.BlockSpec(memory_space=pltpu.SMEM)
    hbm = pl.BlockSpec(memory_space=pltpu.HBM)
    pressure_out, states_out = pl.pallas_call(
        functools.partial(kernel, sizes),
        out_shape=[
            jax.ShapeDtypeStruct((cx, cz, ny), f32),
            jax.ShapeDtypeStruct((slots, filt), f32),
        ],
        in_specs=[hbm, hbm, hbm, hbm, smem, hbm, hbm, hbm, hbm, hbm],
        out_specs=[hbm, hbm],
        scratch_shapes=[
            pltpu.VMEM((cx, cz, ny), f32),
            pltpu.VMEM((slots, filt), f32),
            pltpu.VMEM((1, slots), jnp.int32),
            pltpu.VMEM((1, slots), jnp.int32),
            pltpu.VMEM((1, slots), jnp.int32),
            pltpu.VMEM((kinds, filt, filt), f32),
            pltpu.VMEM((kinds, filt), f32),
            pltpu.VMEM((kinds, filt), f32),
            pltpu.VMEM((2, STEPS + 1, filt, slots), f32),
            pltpu.VMEM((STEPS, 2, 3, filt, slots), f32),
            pltpu.VMEM((2, filt, slots), f32),
            pltpu.VMEM((8, slots), f32),
            pltpu.VMEM((8, slots), f32),
            pltpu.VMEM((STEPS - 1, 1, slots), f32),
            pltpu.VMEM((STEPS - 1, 1, slots), f32),
            pltpu.VMEM((2, kinds, 1, slots), f32),
            pltpu.VMEM((2, 5, slots, slots), bf16),
            pltpu.VMEM((kinds * filt, 2 * filt), bf16),
            pltpu.VMEM((kinds * filt, filt), bf16),
            pltpu.VMEM((2, filt, slots), f32),
            pltpu.VMEM((2, filt, slots), f32),
            pltpu.VMEM((cx, cz, ny), f32),
            pltpu.VMEM((STEPS, cx + 2, cz, ny), f32),
            pltpu.VMEM((STEPS, 2, cx, ny), f32),
            pltpu.VMEM((STEPS, 4, 1, ny), f32),
            pltpu.VMEM((STEPS, 2, cx, ny), f32),
            pltpu.VMEM((STEPS, 4, 1, ny), f32),
            pltpu.VMEM((STEPS, 1, slots), f32),
            pltpu.VMEM((STEPS, 8, 1, slots), f32),
            pltpu.VMEM((3, slots, 128), f32),
            pltpu.VMEM((STEPS, slots, 128), f32),
            pltpu.VMEM((STEPS, cx, cz, ny), f32),
            pltpu.VMEM((slots, 128), f32),
            pltpu.SemaphoreType.DMA((9,)),
            pltpu.SemaphoreType.DMA((4,)),
            pltpu.SemaphoreType.DMA((2,)),
            pltpu.SemaphoreType.DMA((CHUNKS,)),
            pltpu.SemaphoreType.DMA((CHUNKS,)),
            pltpu.SemaphoreType.DMA((STEPS - 1,)),
            pltpu.SemaphoreType.DMA((STEPS - 1,)),
            pltpu.SemaphoreType.DMA((STEPS, 2, 3, CHUNKS)),
            pltpu.SemaphoreType.DMA((STEPS, 2, 3, CHUNKS)),
            pltpu.SemaphoreType.DMA((STEPS, 8)),
            pltpu.SemaphoreType.DMA((STEPS, 8)),
            pltpu.SemaphoreType.DMA((STEPS, 8)),
            pltpu.SemaphoreType.DMA((STEPS, 8)),
        ],
        compiler_params=pltpu.CompilerParams(
            collective_id=0, has_side_effects=True, vmem_limit_bytes=60 * 1024 * 1024
        ),
        name="leapfrog",
    )(
        pressure,
        previous,
        states.reshape(slots, filt),
        wall_cell.reshape(1, slots),
        wall_count,
        material.reshape(1, slots),
        partner.reshape(1, slots),
        transitions,
        inputs,
        outputs,
    )
    pressure_out, states_out = pl.pallas_call(
        hand_over,
        out_shape=[
            jax.ShapeDtypeStruct((cx, cz, ny), f32),
            jax.ShapeDtypeStruct((slots, filt), f32),
        ],
        in_specs=[hbm, hbm],
        out_specs=[hbm, hbm],
        scratch_shapes=[
            pltpu.VMEM((cx, cz, ny), f32),
            pltpu.VMEM((slots, filt), f32),
            pltpu.SemaphoreType.DMA((5,)),
            pltpu.SemaphoreType.DMA((5,)),
        ],
        name="hand_over",
    )(pressure_out, states_out)
    return pressure_out, states_out.reshape(1, 1, slots, filt)


def solution(mesh):
    placed = (
        P("gx", "gz", None),
        P("gx", "gz", None),
        P("gx", "gz", None, None),
        P("gx", "gz", None),
        P("gx", "gz"),
        P("gx", "gz", None),
        P("gx", "gz", None),
        P(),
        P(),
        P(),
    )
    return jax.shard_map(
        per_device,
        mesh=mesh,
        in_specs=placed,
        out_specs=(P("gx", "gz", None), P("gx", "gz", None, None)),
        check_vma=False,
    )
```
